32 devices in a mesh: parts: 2 (over x), train: 8 (over z, y), layer: 2 (over core).
Axes of the slice: x: 2, y: 2, z: 4, core: 2. Of those that a mesh axis runs over, the one named last changes fastest.
Arguments:
- train_inputs: bfloat16 [2, 32, 192, 4096], P('layer', ('parts', 'train')), parts along dimension 1, may hold values from -6 to 6
- train_grads: bfloat16 [2, 32, 192, 4096], P('layer', ('parts', 'train')), parts along dimension 1, may hold values from -6 to 6
- query_inputs: bfloat16 [2, 128, 32, 4096], P('layer', ('parts', 'train')), parts along dimension 1, may hold values from -6 to 6
- query_grads: bfloat16 [2, 128, 32, 4096], P('layer', ('parts', 'train')), parts along dimension 1, may hold values from -6 to 6
- in_project: bfloat16 [2, 4096, 64], P('layer'), may hold values from -0.09375 to 0.09375
- out_project: bfloat16 [2, 4096, 64], P('layer'), may hold values from -0.09375 to 0.09375
- in_factor: float32 [2, 64, 64], P('layer'), as said below
- out_factor: float32 [2, 64, 64], P('layer'), as said below
- train_lengths: int32 [32], P(('parts', 'train')), parts along dimension 0, may hold values from 1 to 192, as said below
- query_lengths: int32 [128], P(('parts', 'train')), parts along dimension 0, may hold values from 1 to 32, as said below
Outputs:
- scores: float32 [32, 64], P(('parts', 'train'), 'layer'), parts along dimension 0
The draws below stay inside these ranges and needn't reach their ends.
There are 2 independent parts, one for each index of `parts`. The reference program is written for one: setup_inputs(seed, part) draws one part's arguments, and reference() takes and returns one part's arrays. A program takes and returns all parts, laid end to end along the dimension named above; an argument that names none is the same for every part. Nothing has to cross between parts.
Inputs may be any that keep to these rules, and one draw needn't show every extreme that they name: `train_lengths`: at least one training sequence has exactly 192 tokens. `query_lengths`: at least one query sequence has exactly 32 tokens. `in_factor`: Symmetric, with each diagonal entry larger than the sum of magnitudes of its row's other entries. `out_factor`: Symmetric, with each diagonal entry larger than the sum of magnitudes of its row's other entries.
All inputs are finite; a program needn't handle non-finite values.
Results may differ from the reference program's by a relative error of at most 0.0043.
Values may be sent and summed in bfloat16 or wider, within the bound.
A program may use at most 64 MiB of HBM per device.

```python
import jax
import jax.numpy as jnp
from jax import lax

D = 4096
RANK = 64
TLEN = 192
QLEN = 32
LAYERS = 2
TRAIN = 16
QUERIES = 64


def dominant_factor(key):
    first, second = jax.random.split(key)
    raw = jax.random.uniform(first, (LAYERS, RANK, RANK), jnp.float32, -1.0, 1.0) / RANK ** 0.5
    symmetric = (raw + jnp.swapaxes(raw, 1, 2)) * 0.5
    eye = jnp.eye(RANK, dtype=jnp.float32)
    off_part = symmetric * (1.0 - eye)
    extra = jnp.exp(jax.random.uniform(second, (LAYERS, RANK), jnp.float32, -0.7, 0.7))
    diagonal = jnp.sum(jnp.abs(off_part), axis=2) + extra
    return off_part + diagonal[:, :, None] * eye


def draw_in_factor(key, part):
    key = jax.random.fold_in(key, 11)
    return dominant_factor(key)


def draw_out_factor(key, part):
    key = jax.random.fold_in(key, 12)
    return dominant_factor(key)


def draw_train_lengths(key, part):
    key = jax.random.fold_in(key, 13)
    first, second = jax.random.split(key)
    values = jax.random.randint(first, (TRAIN,), 1, TLEN + 1)
    where = jax.random.randint(second, (), 0, TRAIN)
    return values.at[where].set(TLEN).astype(jnp.int32)


def draw_query_lengths(key, part):
    key = jax.random.fold_in(key, 14)
    first, second = jax.random.split(key)
    values = jax.random.randint(first, (QUERIES,), 1, QLEN + 1)
    where = jax.random.randint(second, (), 0, QUERIES)
    return values.at[where].set(QLEN).astype(jnp.int32)


def steps_of(key, extent, shards, low, largest):
    level = 1.0
    for position, shards_of in shards:
        heights = jax.random.uniform(jax.random.fold_in(jax.random.fold_in(key, 6), position), (shards_of,), jnp.float32, low / len(shards), largest / len(shards))
        level = level * jnp.repeat(jnp.exp(heights), extent[position] // shards_of).reshape((-1,) + (1,) * (len(extent) - 1 - position))
    return level


def bell_draw(key, shape, scale, reach, cuts=(), kind=jnp.bfloat16):
    result = jax.random.normal(key, shape, jnp.float32) * scale
    if len(cuts) > 0:
        result = steps_of(key, shape, cuts, -0.22, 0.18) * result
    return jnp.clip(result, min=-reach, max=reach).astype(kind)


def setup_inputs(seed: int = 0, part: int = 0) -> dict:
    arg_keys = jax.random.split(jax.random.key(seed), 11)
    part_splits = jax.random.split(jax.random.fold_in(arg_keys[10], part), 11)
    train_inputs = bell_draw(part_splits[0], (LAYERS, TRAIN, TLEN, D), 1.0, 6.0, ((0, 2), (1, 8)))
    train_grads = bell_draw(part_splits[1], (LAYERS, TRAIN, TLEN, D), 1.0, 6.0, ((0, 2), (1, 8)))
    query_inputs = bell_draw(part_splits[2], (LAYERS, QUERIES, QLEN, D), 1.0, 6.0, ((0, 2), (1, 8)))
    query_grads = bell_draw(part_splits[3], (LAYERS, QUERIES, QLEN, D), 1.0, 6.0, ((0, 2), (1, 8)))
    in_project = bell_draw(arg_keys[4], (LAYERS, D, RANK), D ** -0.5, 0.09375, ((0, 2),))
    out_project = bell_draw(arg_keys[5], (LAYERS, D, RANK), D ** -0.5, 0.09375, ((0, 2),))
    in_factor = draw_in_factor(jax.random.fold_in(arg_keys[10], 71), part)
    out_factor = draw_out_factor(jax.random.fold_in(arg_keys[10], 71), part)
    train_lengths = draw_train_lengths(jax.random.fold_in(jax.random.fold_in(arg_keys[10], part), 71), part)
    query_lengths = draw_query_lengths(jax.random.fold_in(jax.random.fold_in(arg_keys[10], part), 71), part)
    return dict(train_inputs=train_inputs, train_grads=train_grads, query_inputs=query_inputs, query_grads=query_grads, in_project=in_project, out_project=out_project, in_factor=in_factor, out_factor=out_factor, train_lengths=train_lengths, query_lengths=query_lengths)


def project(inputs, grads, lengths, in_weight, out_weight):
    xp = jnp.einsum('std,dr->str', inputs.astype(jnp.float32), in_weight.astype(jnp.float32))
    gp = jnp.einsum('std,dr->str', grads.astype(jnp.float32), out_weight.astype(jnp.float32))
    steps = lax.broadcasted_iota(jnp.int32, gp.shape[:2], 1)
    mask = (steps < lengths[:, None]).astype(jnp.float32)
    gp = gp * mask[:, :, None]
    outer = jnp.einsum('sto,sti->soi', gp, xp, precision=lax.Precision.HIGHEST)
    return outer / lengths[:, None, None].astype(jnp.float32)


def reference(train_inputs, train_grads, query_inputs, query_grads, in_project, out_project, in_factor, out_factor, train_lengths, query_lengths):
    total = jnp.zeros((TRAIN, QUERIES), jnp.float32)
    for layer in range(LAYERS):
        train_grad = project(train_inputs[layer], train_grads[layer], train_lengths, in_project[layer], out_project[layer])
        train_vec = train_grad.reshape(TRAIN, RANK * RANK).astype(jnp.bfloat16)
        query_grad = project(query_inputs[layer], query_grads[layer], query_lengths, in_project[layer], out_project[layer])
        conditioned = jnp.einsum('ab,sbc,cd->sad', out_factor[layer], query_grad, in_factor[layer], precision=lax.Precision.HIGHEST)
        query_vec = conditioned.reshape(QUERIES, RANK * RANK).astype(jnp.bfloat16)
        total = total + jnp.dot(train_vec, query_vec.T, preferred_element_type=jnp.float32)
    return total
```

```python
import functools

import jax
import jax.numpy as jnp
from jax import lax
from jax.experimental import pallas as pl
from jax.experimental.pallas import tpu as pltpu
from jax.sharding import PartitionSpec as P

MESH = pl.DeviceIdType.MESH
F32 = jnp.float32
BF16 = jnp.bfloat16
SPLITS = 4


def dot_nt(a, b):
    return lax.dot_general(a, b, (((1,), (1,)), ((), ())), preferred_element_type=F32)


def dot_nn(a, b):
    return lax.dot_general(a, b, (((1,), (0,)), ((), ())), preferred_element_type=F32)


def halves(a):
    high = a.astype(BF16)
    return high, (a - high.astype(F32)).astype(BF16)


def fine(dot, a, b):
    return dot(a[0], b[0]) + (dot(a[0], b[1]) + dot(a[1], b[0]))


def lanes(shape):
    return lax.broadcasted_iota(jnp.int32, shape, len(shape) - 1)


def repeat(count, body):
    if count <= 8:
        for step in range(count):
            body(step)
    else:
        lax.fori_loop(0, count, lambda step, carry: (body(step), carry)[1], 0)


def kernel(
    n,
    xt, gt, xq, gq, win, wout, fin, fout, lt, lq,
    out,
    xt_v, gt_v, xq_v, gq_v, win_v, wout_v, fin_v, fout_v, lt_s, lq_s,
    held, wide, query, mine, landed,
    in_sem, far_sem, small_sem, send_one, recv_one, send_two, recv_two,
):
    trains, slots, width = xt.shape
    queries = lq.shape[0]
    short = xq.shape[0] // queries
    rank = win.shape[0]
    tokens = queries * short
    part = width // SPLITS
    me, layer = lax.axis_index("train"), lax.axis_index("layer")
    half = n // 2
    owner = me // half
    place = lax.rem(me, half)

    small = [
        pltpu.make_async_copy(src, dst, small_sem.at[k])
        for k, (src, dst) in enumerate(((lt, lt_s), (lq, lq_s), (fin, fin_v), (fout, fout_v)))
    ]
    load_win = pltpu.make_async_copy(win, win_v, in_sem.at[0])
    load_wout = pltpu.make_async_copy(wout, wout_v, in_sem.at[1])
    load_x = [pltpu.make_async_copy(xt.at[s], xt_v.at[s], in_sem.at[2 + 2 * s]) for s in range(trains)]
    load_g = [pltpu.make_async_copy(gt.at[s], gt_v.at[s], in_sem.at[3 + 2 * s]) for s in range(trains)]
    cut = [pl.ds(k * part, part) for k in range(SPLITS)]
    load_gq = [pltpu.make_async_copy(gq.at[:, c], gq_v.at[:, c], far_sem.at[k]) for k, c in enumerate(cut)]
    load_xq = [pltpu.make_async_copy(xq.at[:, c], xq_v.at[:, c], far_sem.at[SPLITS + k]) for k, c in enumerate(cut)]
    load_win.start()
    load_x[0].start()
    load_wout.start()
    load_g[0].start()
    for copy in small:
        copy.start()
    for s in range(1, trains):
        load_x[s].start()
        load_g[s].start()
    for copy in load_gq + load_xq:
        copy.start()

    barrier = pltpu.get_barrier_semaphore()

    def greet(step):
        for other in range(2):
            @pl.when(jnp.logical_or(step != me, other != layer))
            def _():
                pl.semaphore_signal(
                    barrier, inc=1, device_id={"train": step, "layer": other}, device_id_type=MESH
                )

    repeat(n, greet)

    for s in range(trains):
        if s == 0:
            load_win.wait()
        load_x[s].wait()
        xp = dot_nt(win_v[...], xt_v[s])
        if s == 0:
            load_wout.wait()
        load_g[s].wait()
        gp = dot_nt(wout_v[...], gt_v[s])
        if s == 0:
            for copy in small:
                copy.wait()
        length = jnp.full((1, slots), lt_s[s], jnp.int32)
        scale = jnp.where(lanes((1, slots)) < length, 1.0 / length.astype(F32), 0.0)
        both = fine(dot_nt, halves(gp * scale), halves(jnp.concatenate([xp, xp], axis=0)))
        packed = jnp.where(lanes((rank // 2, 2 * rank)) < rank, both[: rank // 2], both[rank // 2 :])
        held[me, s] = packed.astype(BF16)

    pl.semaphore_wait(barrier, 2 * n - 1)

    def first(slot, peer, k):
        return pltpu.make_async_remote_copy(
            src_ref=held.at[slot],
            dst_ref=held.at[slot],
            send_sem=send_one.at[k],
            recv_sem=recv_one.at[slot],
            device_id={"train": peer},
            device_id_type=MESH,
        )

    def send_first(k):
        first(me, lax.rem(me + 1 + k, n), k).start()

    repeat(n - 1, send_first)

    token = lanes((1, tokens))
    length = jnp.full((1, tokens), lq_s[0], jnp.int32)
    for j in range(1, queries):
        length = jnp.where(token // short == j, lq_s[j], length)
    scale = jnp.where(lax.rem(token, short) < length, 1.0 / length.astype(F32), 0.0)
    gp = jnp.zeros((rank, tokens), F32)
    for k, c in enumerate(cut):
        load_gq[k].wait()
        gp += dot_nt(wout_v[:, c], gq_v[:, c])
    gp = fine(dot_nn, halves(fout_v[...]), halves(gp * scale))
    block = (
        lanes((1, queries, tokens)) // short == lax.broadcasted_iota(jnp.int32, (1, queries, tokens), 1)
    ).astype(F32)
    spread = halves((gp[:, None, :] * block).reshape(rank * queries, tokens))
    xp = jnp.zeros((rank, tokens), F32)
    for k, c in enumerate(cut):
        load_xq[k].wait()
        xp += dot_nt(win_v[:, c], xq_v[:, c])
    xp = fine(dot_nn, halves(fin_v[...]), halves(xp))
    both = fine(dot_nt, spread, halves(jnp.concatenate([xp, xp], axis=0)))
    rows = rank // 2 * queries
    query[...] = (
        jnp.where(lanes((rows, 2 * rank)) < rank, both[:rows], both[rows:]).astype(BF16).astype(F32)
    )

    def second(peer, to, where, source, k):
        return pltpu.make_async_remote_copy(
            src_ref=mine.at[k],
            dst_ref=landed.at[where, source],
            send_sem=send_two.at[k],
            recv_sem=recv_two.at[where, source],
            device_id={"train": peer, "layer": to},
            device_id_type=MESH,
        )

    def own(k):
        return pltpu.make_async_copy(mine.at[k], landed.at[place, layer], recv_two.at[place, layer])

    def score(k):
        peer = lax.rem(me + 1 + k, n)
        if isinstance(k, int):
            if k < n - 1:
                first(peer, peer, k).wait_recv()
        else:
            @pl.when(k < n - 1)
            def _():
                first(peer, peer, k).wait_recv()
        sums = []
        for s in range(trains):
            wide[...] = held[peer, s].astype(F32)
            total = jnp.zeros((queries, 2 * rank), F32)
            for a in range(rank // 2):
                total += wide[a : a + 1, :] * query[a * queries : (a + 1) * queries, :]
            sums.append(total + pltpu.roll(total, rank, 1))
        mine[k] = jnp.where(lanes((queries, 2 * rank)) < rank, sums[0], sums[1])
        local = jnp.logical_and(peer == me, owner == layer)

        @pl.when(jnp.logical_not(local))
        def _():
            second(peer, owner, place, layer, k).start()

        @pl.when(local)
        def _():
            own(k).start()

    repeat(n, score)

    def collect(where):
        for source in range(2):
            origin = layer * half + where
            local = jnp.logical_and(origin == me, source == layer)

            @pl.when(jnp.logical_not(local))
            def _():
                second(me, layer, where, source, 0).wait_recv()

            @pl.when(local)
            def _():
                own(n - 1).wait()

    repeat(half, collect)
    total = (landed[:, 0] + landed[:, 1]).reshape(half * queries, 2 * rank)
    high, low = halves(total)
    rest = (total - high.astype(F32) - low.astype(F32)).astype(BF16)
    pick = (
        lanes((8, 2 * rank)) // rank == lax.broadcasted_iota(jnp.int32, (8, 2 * rank), 0)
    ).astype(F32).astype(BF16)
    result = dot_nt(pick, high) + (dot_nt(pick, low) + dot_nt(pick, rest))
    out[...] = result[:trains]

    def finish_first(k):
        first(me, lax.rem(me + 1 + k, n), k).wait_send()

    repeat(n - 1, finish_first)

    def finish_second(k):
        peer = lax.rem(me + 1 + k, n)

        @pl.when(jnp.logical_not(jnp.logical_and(peer == me, owner == layer)))
        def _():
            second(peer, owner, place, layer, k).wait_send()

    repeat(n, finish_second)


def on_device(n, xt, gt, xq, gq, win, wout, fin, fout, lt, lq):
    _, trains, slots, width = xt.shape
    _, queries, short, _ = xq.shape
    rank = win.shape[2]
    tokens = queries * short
    half = n // 2
    return pl.pallas_call(
        functools.partial(kernel, n),
        out_shape=jax.ShapeDtypeStruct((trains, half * queries), F32),
        in_specs=[pl.BlockSpec(memory_space=pl.ANY)] * 10,
        out_specs=pl.BlockSpec(memory_space=pltpu.VMEM),
        scratch_shapes=[
            pltpu.VMEM((trains, slots, width), BF16),
            pltpu.VMEM((trains, slots, width), BF16),
            pltpu.VMEM((tokens, width), BF16),
            pltpu.VMEM((tokens, width), BF16),
            pltpu.VMEM((rank, width), BF16),
            pltpu.VMEM((rank, width), BF16),
            pltpu.VMEM((rank, rank), F32),
            pltpu.VMEM((rank, rank), F32),
            pltpu.SMEM((trains,), jnp.int32),
            pltpu.SMEM((queries,), jnp.int32),
            pltpu.VMEM((n, trains, rank // 2, 2 * rank), BF16),
            pltpu.VMEM((rank // 2, 2 * rank), F32),
            pltpu.VMEM((rank // 2 * queries, 2 * rank), F32),
            pltpu.VMEM((n, queries, 2 * rank), F32),
            pltpu.VMEM((half, 2, queries, 2 * rank), F32),
            pltpu.SemaphoreType.DMA((2 + 2 * trains,)),
            pltpu.SemaphoreType.DMA((2 * SPLITS,)),
            pltpu.SemaphoreType.DMA((4,)),
            pltpu.SemaphoreType.DMA((n,)),
            pltpu.SemaphoreType.DMA((n,)),
            pltpu.SemaphoreType.DMA((n,)),
            pltpu.SemaphoreType.DMA((half, 2)),
        ],
        compiler_params=pltpu.CompilerParams(
            collective_id=0, has_side_effects=True, vmem_limit_bytes=48 * 1024 * 1024
        ),
        cost_estimate=pl.CostEstimate(
            flops=4 * (trains * slots + tokens) * width * rank,
            bytes_accessed=4 * (trains * slots + tokens + rank) * width,
            transcendentals=0,
        ),
    )(
        xt[0], gt[0], xq.reshape(tokens, width), gq.reshape(tokens, width),
        win[0].T, wout[0].T, fin[0], fout[0], lt, lq,
    )


def solution(mesh):
    rows = P("layer", ("parts", "train"), None, None)
    shared = P("layer", None, None)
    counts = P(("parts", "train"))
    return jax.shard_map(
        functools.partial(on_device, mesh.shape["train"]),
        mesh=mesh,
        in_specs=(rows,) * 4 + (shared,) * 4 + (counts,) * 2,
        out_specs=P(("parts", "train"), "layer"),
        check_vma=False,
    )
```

```python
import functools

import jax
import jax.numpy as jnp
from jax import lax
from jax.experimental import pallas as pl
from jax.experimental.pallas import tpu as pltpu
from jax.sharding import PartitionSpec as P

MESH = pl.DeviceIdType.MESH
F32 = jnp.float32
BF16 = jnp.bfloat16
SPLITS = 4


def dot_nt(a, b):
    return lax.dot_general(a, b, (((1,), (1,)), ((), ())), preferred_element_type=F32)


def dot_nn(a, b):
    return lax.dot_general(a, b, (((1,), (0,)), ((), ())), preferred_element_type=F32)


def halves(a):
    high = a.astype(BF16)
    return high, (a - high.astype(F32)).astype(BF16)


def fine(dot, a, b):
    return dot(a[0], b[0]) + (dot(a[0], b[1]) + dot(a[1], b[0]))


def lanes(shape):
    return lax.broadcasted_iota(jnp.int32, shape, len(shape) - 1)


def rows_of(shape):
    return lax.broadcasted_iota(jnp.int32, shape, 0)


def repeat(count, body):
    if count <= 8:
        for step in range(count):
            body(step)
    else:
        lax.fori_loop(0, count, lambda step, carry: (body(step), carry)[1], 0)


def kernel(
    n,
    xt, gt, xq, gq, win, wout, fin, fout, lt, lq,
    out,
    xt_v, gt_v, xq_v, gq_v, win_v, wout_v, fin_v, fout_v, lt_s, lq_s,
    held, wide, wide_query, query, mine, landed,
    in_sem, far_sem, small_sem, send_one, recv_one, send_two, recv_two,
):
    trains, slots, width = xt.shape
    queries = lq.shape[0]
    short = xq.shape[0] // queries
    rank = win.shape[0]
    tokens = queries * short
    part = width // SPLITS
    me, layer = lax.axis_index("train"), lax.axis_index("layer")
    half = n // 2
    owner = me // half
    place = lax.rem(me, half)

    small = [
        pltpu.make_async_copy(src, dst, small_sem.at[k])
        for k, (src, dst) in enumerate(((lt, lt_s), (lq, lq_s), (fin, fin_v), (fout, fout_v)))
    ]
    load_win = pltpu.make_async_copy(win, win_v, in_sem.at[0])
    load_wout = pltpu.make_async_copy(wout, wout_v, in_sem.at[1])
    load_x = [pltpu.make_async_copy(xt.at[s], xt_v.at[s], in_sem.at[2 + 2 * s]) for s in range(trains)]
    load_g = [pltpu.make_async_copy(gt.at[s], gt_v.at[s], in_sem.at[3 + 2 * s]) for s in range(trains)]
    cut = [pl.ds(k * part, part) for k in range(SPLITS)]
    load_gq = [pltpu.make_async_copy(gq.at[:, c], gq_v.at[:, c], far_sem.at[k]) for k, c in enumerate(cut)]
    load_xq = [pltpu.make_async_copy(xq.at[:, c], xq_v.at[:, c], far_sem.at[SPLITS + k]) for k, c in enumerate(cut)]
    for copy in [load_win, load_x[0], load_wout, load_g[0]] + small:
        copy.start()

    barrier = pltpu.get_barrier_semaphore()

    def greet(step):
        for other in range(2):
            @pl.when(jnp.logical_or(step != me, other != layer))
            def _():
                pl.semaphore_signal(
                    barrier, inc=1, device_id={"train": step, "layer": other}, device_id_type=MESH
                )

    repeat(n, greet)

    def first(slot, s, peer, k):
        return pltpu.make_async_remote_copy(
            src_ref=held.at[slot, s],
            dst_ref=held.at[slot, s],
            send_sem=send_one.at[k, s],
            recv_sem=recv_one.at[slot, s],
            device_id={"train": peer},
            device_id_type=MESH,
        )

    for s in range(trains):
        if s == 0:
            load_win.wait()
        load_x[s].wait()
        for copy in [load_x[s + 1]] if s + 1 < trains else load_gq:
            copy.start()
        xp = dot_nt(win_v[...], xt_v[s])
        if s == 0:
            load_wout.wait()
        load_g[s].wait()
        for copy in [load_g[s + 1]] if s + 1 < trains else load_xq:
            copy.start()
        gp = dot_nt(wout_v[...], gt_v[s])
        if s == 0:
            for copy in small:
                copy.wait()
        step = lanes((rank, slots))
        length = jnp.full((rank, slots), lt_s[s], jnp.int32)
        gp = jnp.where(step < length, gp / length.astype(F32), 0.0)
        both = fine(dot_nt, halves(gp), halves(jnp.concatenate([xp, xp], axis=0)))
        packed = jnp.where(lanes((rank // 2, 2 * rank)) < rank, both[: rank // 2], both[rank // 2 :])
        held[me, s] = packed.astype(BF16)
        if s == 0:
            pl.semaphore_wait(barrier, 2 * n - 1)

        def send_first(k):
            first(me, s, lax.rem(me + 1 + k, n), k).start()

        repeat(n - 1, send_first)

    step = lanes((1, tokens))
    length = jnp.full((1, tokens), lq_s[0], jnp.int32)
    for j in range(1, queries):
        length = jnp.where(step >= j * short, lq_s[j], length)
    scale = jnp.where(lax.rem(step, short) < length, 1.0 / length.astype(F32), 0.0)
    gp = jnp.zeros((rank, tokens), F32)
    for k, c in enumerate(cut):
        load_gq[k].wait()
        gp += dot_nt(wout_v[:, c], gq_v[:, c])
    gp = fine(dot_nn, halves(fout_v[...]), halves(gp * scale))
    blocks = [
        jnp.logical_and(step >= j * short, step < (j + 1) * short).astype(F32) for j in range(queries)
    ]
    spread = [
        jnp.concatenate([(term.astype(F32) * block).astype(BF16) for block in blocks], axis=0)
        for term in halves(gp)
    ]
    xp = jnp.zeros((rank, tokens), F32)
    for k, c in enumerate(cut):
        load_xq[k].wait()
        xp += dot_nt(win_v[:, c], xq_v[:, c])
    factor = fin_v[...]
    xp = fine(dot_nn, halves(jnp.concatenate([factor, factor], axis=0)), halves(xp))
    wide_query[...] = fine(dot_nt, spread, halves(xp))
    left = lanes((queries, 2 * rank)) < rank
    for a in range(rank // 2):
        row = jnp.where(
            left,
            wide_query[pl.ds(a, queries, rank), :],
            wide_query[pl.ds(a + rank // 2, queries, rank), :],
        )
        query[a * queries : (a + 1) * queries, :] = row.astype(BF16).astype(F32)

    def second(peer, to, where, source, k):
        return pltpu.make_async_remote_copy(
            src_ref=mine.at[k],
            dst_ref=landed.at[where, source],
            send_sem=send_two.at[k],
            recv_sem=recv_two.at[where, source],
            device_id={"train": peer, "layer": to},
            device_id_type=MESH,
        )

    def own(k):
        return pltpu.make_async_copy(mine.at[k], landed.at[place, layer], recv_two.at[place, layer])

    def score(peer):
        @pl.when(peer != me)
        def _():
            for s in range(trains):
                first(peer, s, peer, 0).wait_recv()

        sums = []
        for s in range(trains):
            wide[...] = held[peer, s].astype(F32)
            total = jnp.zeros((queries, 2 * rank), F32)
            for a in range(rank // 2):
                total += wide[a : a + 1, :] * query[a * queries : (a + 1) * queries, :]
            sums.append(total + pltpu.roll(total, rank, 1))
        mine[peer] = jnp.where(lanes((queries, 2 * rank)) < rank, sums[0], sums[1])
        local = jnp.logical_and(peer == me, owner == layer)

        @pl.when(jnp.logical_not(local))
        def _():
            second(peer, owner, place, layer, peer).start()

        @pl.when(local)
        def _():
            own(peer).start()

    repeat(n, score)

    def collect(where):
        for source in range(2):
            origin = layer * half + where
            local = jnp.logical_and(origin == me, source == layer)

            @pl.when(jnp.logical_not(local))
            def _():
                second(me, layer, where, source, 0).wait_recv()

            @pl.when(local)
            def _():
                own(me).wait()

    repeat(half, collect)
    total = (landed[:, 0] + landed[:, 1]).reshape(half * queries, 2 * rank)
    high, low = halves(total)
    rest = (total - high.astype(F32) - low.astype(F32)).astype(BF16)
    pick = (
        lanes((8, 2 * rank)) // rank == lax.broadcasted_iota(jnp.int32, (8, 2 * rank), 0)
    ).astype(F32).astype(BF16)
    result = dot_nt(pick, high) + (dot_nt(pick, low) + dot_nt(pick, rest))
    out[...] = result[:trains]

    def finish_first(k):
        for s in range(trains):
            first(me, s, lax.rem(me + 1 + k, n), k).wait_send()

    repeat(n - 1, finish_first)

    def finish_second(peer):
        @pl.when(jnp.logical_not(jnp.logical_and(peer == me, owner == layer)))
        def _():
            second(peer, owner, place, layer, peer).wait_send()

    repeat(n, finish_second)


def on_device(n, xt, gt, xq, gq, win, wout, fin, fout, lt, lq):
    _, trains, slots, width = xt.shape
    _, queries, short, _ = xq.shape
    rank = win.shape[2]
    tokens = queries * short
    half = n // 2
    return pl.pallas_call(
        functools.partial(kernel, n),
        out_shape=jax.ShapeDtypeStruct((trains, half * queries), F32),
        in_specs=[pl.BlockSpec(memory_space=pltpu.HBM)] * 10,
        out_specs=pl.BlockSpec(memory_space=pltpu.VMEM),
        scratch_shapes=[
            pltpu.VMEM((trains, slots, width), BF16),
            pltpu.VMEM((trains, slots, width), BF16),
            pltpu.VMEM((tokens, width), BF16),
            pltpu.VMEM((tokens, width), BF16),
            pltpu.VMEM((rank, width), BF16),
            pltpu.VMEM((rank, width), BF16),
            pltpu.VMEM((rank, rank), F32),
            pltpu.VMEM((rank, rank), F32),
            pltpu.SMEM((trains,), jnp.int32),
            pltpu.SMEM((queries,), jnp.int32),
            pltpu.VMEM((n, trains, rank // 2, 2 * rank), BF16),
            pltpu.VMEM((rank // 2, 2 * rank), F32),
            pltpu.VMEM((rank * queries, 2 * rank), F32),
            pltpu.VMEM((rank // 2 * queries, 2 * rank), F32),
            pltpu.VMEM((n, queries, 2 * rank), F32),
            pltpu.VMEM((half, 2, queries, 2 * rank), F32),
            pltpu.SemaphoreType.DMA((2 + 2 * trains,)),
            pltpu.SemaphoreType.DMA((2 * SPLITS,)),
            pltpu.SemaphoreType.DMA((4,)),
            pltpu.SemaphoreType.DMA((n, trains)),
            pltpu.SemaphoreType.DMA((n, trains)),
            pltpu.SemaphoreType.DMA((n,)),
            pltpu.SemaphoreType.DMA((half, 2)),
        ],
        compiler_params=pltpu.CompilerParams(
            collective_id=0, has_side_effects=True, vmem_limit_bytes=63 * 1024 * 1024
        ),
        cost_estimate=pl.CostEstimate(
            flops=4 * (trains * slots + tokens) * width * rank,
            bytes_accessed=4 * (trains * slots + tokens + rank) * width,
            transcendentals=0,
        ),
    )(
        xt[0], gt[0], xq.reshape(tokens, width), gq.reshape(tokens, width),
        win[0].T, wout[0].T, fin[0], fout[0], lt, lq,
    )


def solution(mesh):
    rows = P("layer", ("parts", "train"), None, None)
    shared = P("layer", None, None)
    counts = P(("parts", "train"))
    return jax.shard_map(
        functools.partial(on_device, mesh.shape["train"]),
        mesh=mesh,
        in_specs=(rows,) * 4 + (shared,) * 4 + (counts,) * 2,
        out_specs=P(("parts", "train"), "layer"),
        check_vma=False,
    )
```

```python
import functools

import jax
import jax.numpy as jnp
from jax import lax
from jax.experimental import pallas as pl
from jax.experimental.pallas import tpu as pltpu
from jax.sharding import PartitionSpec as P

MESH = pl.DeviceIdType.MESH
F32 = jnp.float32
BF16 = jnp.bfloat16
SPLITS = 4


def dot_nt(a, b):
    return lax.dot_general(a, b, (((1,), (1,)), ((), ())), preferred_element_type=F32)


def dot_nn(a, b):
    return lax.dot_general(a, b, (((1,), (0,)), ((), ())), preferred_element_type=F32)


def halves(a):
    high = a.astype(BF16)
    return high, (a - high.astype(F32)).astype(BF16)


def fine(dot, a, b):
    return dot(a[0], b[0]) + (dot(a[0], b[1]) + dot(a[1], b[0]))


def lanes(shape):
    return lax.broadcasted_iota(jnp.int32, shape, len(shape) - 1)


def rows_of(shape):
    return lax.broadcasted_iota(jnp.int32, shape, 0)


def repeat(count, body):
    if count <= 8:
        for step in range(count):
            body(step)
    else:
        lax.fori_loop(0, count, lambda step, carry: (body(step), carry)[1], 0)


def kernel(
    n,
    xt, gt, xq, gq, win, wout, fin, fout, lt, lq,
    out,
    xt_v, gt_v, xq_v, gq_v, win_v, wout_v, fin_v, fout_v, lt_s, lq_s,
    held, wide, wide_query, query, mine, landed,
    in_sem, far_sem, small_sem, send_one, recv_one, send_two, recv_two,
):
    trains, slots, width = xt.shape
    queries = lq.shape[0]
    short = xq.shape[0] // queries
    rank = win.shape[0]
    tokens = queries * short
    part = width // SPLITS
    me, layer = lax.axis_index("train"), lax.axis_index("layer")
    half = n // 2
    owner = me // half
    place = lax.rem(me, half)

    small = [
        pltpu.make_async_copy(src, dst, small_sem.at[k])
        for k, (src, dst) in enumerate(((lt, lt_s), (lq, lq_s), (fin, fin_v), (fout, fout_v)))
    ]
    cut = [pl.ds(k * part, part) for k in range(SPLITS)]

    def pieces(src, dst, base):
        return [pltpu.make_async_copy(src.at[:, c], dst.at[:, c], in_sem.at[base, k]) for k, c in enumerate(cut)]

    load_win = pieces(win, win_v, 0)
    load_wout = pieces(wout, wout_v, 1)
    load_x = [pieces(xt.at[s], xt_v.at[s], 2 + 2 * s) for s in range(trains)]
    load_g = [pieces(gt.at[s], gt_v.at[s], 3 + 2 * s) for s in range(trains)]
    load_gq = [pltpu.make_async_copy(gq.at[:, c], gq_v.at[:, c], far_sem.at[k]) for k, c in enumerate(cut)]
    load_xq = [pltpu.make_async_copy(xq.at[:, c], xq_v.at[:, c], far_sem.at[SPLITS + k]) for k, c in enumerate(cut)]
    for pair in list(zip(load_win, load_x[0])) + list(zip(load_wout, load_g[0])) + [small] + load_x[1:] + load_g[1:]:
        for copy in pair:
            copy.start()

    barrier = pltpu.get_barrier_semaphore()

    def greet(step):
        for other in range(2):
            @pl.when(jnp.logical_or(step != me, other != layer))
            def _():
                pl.semaphore_signal(
                    barrier, inc=1, device_id={"train": step, "layer": other}, device_id_type=MESH
                )

    repeat(n, greet)

    def first(slot, s, peer, k):
        return pltpu.make_async_remote_copy(
            src_ref=held.at[slot, s],
            dst_ref=held.at[slot, s],
            send_sem=send_one.at[k, s],
            recv_sem=recv_one.at[slot, s],
            device_id={"train": peer},
            device_id_type=MESH,
        )

    def project(weight, rows, copies):
        total = jnp.zeros((rank, rows.shape[0]), F32)
        for k, c in enumerate(cut):
            for copy in copies[k]:
                copy.wait()
            total += dot_nt(weight[:, c], rows[:, c])
        return total

    def gradient(s, xp, gp):
        length = jnp.full((rank, slots), lt_s[s], jnp.int32)
        gp = jnp.where(lanes((rank, slots)) < length, gp / length.astype(F32), 0.0)
        both = fine(dot_nt, halves(gp), halves(jnp.concatenate([xp, xp], axis=0)))
        packed = jnp.where(lanes((rank // 2, 2 * rank)) < rank, both[: rank // 2], both[rank // 2 :])
        held[me, s] = packed.astype(BF16)

    def send_gradient(s):
        def send_first(k):
            first(me, s, lax.rem(me + 1 + k, n), k).start()

        repeat(n - 1, send_first)

    for s in range(trains):
        if s == 0:
            xp = project(win_v, xt_v.at[s], list(zip(load_win, load_x[s])))
            for copy in load_gq + load_xq:
                copy.start()
            gp = project(wout_v, gt_v.at[s], list(zip(load_wout, load_g[s])))
            for copy in small:
                copy.wait()
        else:
            for copy in load_x[s]:
                copy.wait()
            later = dot_nt(win_v[...], xt_v[s])
            gradient(s - 1, xp, gp)
            if s == 1:
                pl.semaphore_wait(barrier, 2 * n - 1)
            send_gradient(s - 1)
            xp = later
            gp = project(wout_v, gt_v.at[s], [[copy] for copy in load_g[s]])
    gradient(trains - 1, xp, gp)
    send_gradient(trains - 1)

    step = lanes((1, tokens))
    length = jnp.full((1, tokens), lq_s[0], jnp.int32)
    for j in range(1, queries):
        length = jnp.where(step >= j * short, lq_s[j], length)
    scale = jnp.where(lax.rem(step, short) < length, 1.0 / length.astype(F32), 0.0)
    gp = jnp.zeros((rank, tokens), F32)
    for k, c in enumerate(cut):
        load_gq[k].wait()
        gp += dot_nt(wout_v[:, c], gq_v[:, c])
    gp = fine(dot_nn, halves(fout_v[...]), halves(gp * scale))
    blocks = [
        jnp.logical_and(step >= j * short, step < (j + 1) * short).astype(F32) for j in range(queries)
    ]
    spread = [
        jnp.concatenate([(term.astype(F32) * block).astype(BF16) for block in blocks], axis=0)
        for term in halves(gp)
    ]
    xp = jnp.zeros((rank, tokens), F32)
    for k, c in enumerate(cut):
        load_xq[k].wait()
        xp += dot_nt(win_v[:, c], xq_v[:, c])
    factor = fin_v[...]
    xp = fine(dot_nn, halves(jnp.concatenate([factor, factor], axis=0)), halves(xp))
    wide_query[...] = fine(dot_nt, spread, halves(xp))
    left = lanes((queries, 2 * rank)) < rank
    for a in range(rank // 2):
        row = jnp.where(
            left,
            wide_query[pl.ds(a, queries, rank), :],
            wide_query[pl.ds(a + rank // 2, queries, rank), :],
        )
        query[a * queries : (a + 1) * queries, :] = row.astype(BF16).astype(F32)

    def second(peer, to, where, source, k):
        return pltpu.make_async_remote_copy(
            src_ref=mine.at[k],
            dst_ref=landed.at[where, source],
            send_sem=send_two.at[k],
            recv_sem=recv_two.at[where, source],
            device_id={"train": peer, "layer": to},
            device_id_type=MESH,
        )

    def own(k):
        return pltpu.make_async_copy(mine.at[k], landed.at[place, layer], recv_two.at[place, layer])

    def score(peer):
        @pl.when(peer != me)
        def _():
            for s in range(trains):
                first(peer, s, peer, 0).wait_recv()

        sums = []
        for s in range(trains):
            wide[...] = held[peer, s].astype(F32)
            total = jnp.zeros((queries, 2 * rank), F32)
            for a in range(rank // 2):
                total += wide[a : a + 1, :] * query[a * queries : (a + 1) * queries, :]
            sums.append(total + pltpu.roll(total, rank, 1))
        mine[peer] = jnp.where(lanes((queries, 2 * rank)) < rank, sums[0], sums[1])
        local = jnp.logical_and(peer == me, owner == layer)

        @pl.when(jnp.logical_not(local))
        def _():
            second(peer, owner, place, layer, peer).start()

        @pl.when(local)
        def _():
            own(peer).start()

    repeat(n, score)

    def collect(where):
        for source in range(2):
            origin = layer * half + where
            local = jnp.logical_and(origin == me, source == layer)

            @pl.when(jnp.logical_not(local))
            def _():
                second(me, layer, where, source, 0).wait_recv()

            @pl.when(local)
            def _():
                own(me).wait()

    repeat(half, collect)
    total = (landed[:, 0] + landed[:, 1]).reshape(half * queries, 2 * rank)
    high, low = halves(total)
    rest = (total - high.astype(F32) - low.astype(F32)).astype(BF16)
    pick = (
        lanes((8, 2 * rank)) // rank == lax.broadcasted_iota(jnp.int32, (8, 2 * rank), 0)
    ).astype(F32).astype(BF16)
    result = dot_nt(pick, high) + (dot_nt(pick, low) + dot_nt(pick, rest))
    out[...] = result[:trains]

    def finish_first(k):
        for s in range(trains):
            first(me, s, lax.rem(me + 1 + k, n), k).wait_send()

    repeat(n - 1, finish_first)

    def finish_second(peer):
        @pl.when(jnp.logical_not(jnp.logical_and(peer == me, owner == layer)))
        def _():
            second(peer, owner, place, layer, peer).wait_send()

    repeat(n, finish_second)


def on_device(n, xt, gt, xq, gq, win, wout, fin, fout, lt, lq):
    _, trains, slots, width = xt.shape
    _, queries, short, _ = xq.shape
    rank = win.shape[2]
    tokens = queries * short
    half = n // 2
    return pl.pallas_call(
        functools.partial(kernel, n),
        out_shape=jax.ShapeDtypeStruct((trains, half * queries), F32),
        in_specs=[pl.BlockSpec(memory_space=pltpu.HBM)] * 10,
        out_specs=pl.BlockSpec(memory_space=pltpu.VMEM),
        scratch_shapes=[
            pltpu.VMEM((trains, slots, width), BF16),
            pltpu.VMEM((trains, slots, width), BF16),
            pltpu.VMEM((tokens, width), BF16),
            pltpu.VMEM((tokens, width), BF16),
            pltpu.VMEM((rank, width), BF16),
            pltpu.VMEM((rank, width), BF16),
            pltpu.VMEM((rank, rank), F32),
            pltpu.VMEM((rank, rank), F32),
            pltpu.SMEM((trains,), jnp.int32),
            pltpu.SMEM((queries,), jnp.int32),
            pltpu.VMEM((n, trains, rank // 2, 2 * rank), BF16),
            pltpu.VMEM((rank // 2, 2 * rank), F32),
            pltpu.VMEM((rank * queries, 2 * rank), F32),
            pltpu.VMEM((rank // 2 * queries, 2 * rank), F32),
            pltpu.VMEM((n, queries, 2 * rank), F32),
            pltpu.VMEM((half, 2, queries, 2 * rank), F32),
            pltpu.SemaphoreType.DMA((2 + 2 * trains, SPLITS)),
            pltpu.SemaphoreType.DMA((2 * SPLITS,)),
            pltpu.SemaphoreType.DMA((4,)),
            pltpu.SemaphoreType.DMA((n, trains)),
            pltpu.SemaphoreType.DMA((n, trains)),
            pltpu.SemaphoreType.DMA((n,)),
            pltpu.SemaphoreType.DMA((half, 2)),
        ],
        compiler_params=pltpu.CompilerParams(
            collective_id=0, has_side_effects=True, vmem_limit_bytes=63 * 1024 * 1024
        ),
        cost_estimate=pl.CostEstimate(
            flops=4 * (trains * slots + tokens) * width * rank,
            bytes_accessed=4 * (trains * slots + tokens + rank) * width,
            transcendentals=0,
        ),
    )(
        xt[0], gt[0], xq.reshape(tokens, width), gq.reshape(tokens, width),
        win[0].T, wout[0].T, fin[0], fout[0], lt, lq,
    )


def solution(mesh):
    rows = P("layer", ("parts", "train"), None, None)
    shared = P("layer", None, None)
    counts = P(("parts", "train"))
    return jax.shard_map(
        functools.partial(on_device, mesh.shape["train"]),
        mesh=mesh,
        in_specs=(rows,) * 4 + (shared,) * 4 + (counts,) * 2,
        out_specs=P(("parts", "train"), "layer"),
        check_vma=False,
    )
```
